32 devices in a mesh: groups: 2 (over x), seq: 16 (over z, y, core).
Axes of the slice: x: 2, y: 2, z: 4, core: 2. Of those that a mesh axis runs over, the one named last changes fastest.
Arguments:
- tenant_ids: int32 [8], P('groups'), parts along dimension 0, may hold values from 0 to 15
- timesteps: int32 [8], P('groups'), parts along dimension 0, may hold values from 0 to 999
- counts: int32 [32], P(('groups', 'seq')), parts along dimension 0, may hold values from 1 to 16
- hidden_in: bfloat16 [8, 1024, 3072], P('groups', 'seq'), parts along dimension 0, may hold values from -6 to 6
- frozen_query: bfloat16 [8, 1024, 3072], P('groups', 'seq'), parts along dimension 0, may hold values from -6 to 6
- key_base: bfloat16 [8, 1024, 3072], P('groups', 'seq'), parts along dimension 0, may hold values from -6 to 6
- frozen_value: bfloat16 [8, 1024, 3072], P('groups', 'seq'), parts along dimension 0, may hold values from -6 to 6
- out_grad: bfloat16 [8, 1024, 3072], P('groups', 'seq'), parts along dimension 0, may hold values from -6 to 6
- adapters: float32 [32, 4, 64, 3072], P(('groups', 'seq')), parts along dimension 0, may hold values from -0.625 to 0.625
- first_moment: float32 [32, 4, 64, 3072], P(('groups', 'seq')), parts along dimension 0, may hold values from -4 to 4
- second_moment: float32 [32, 4, 64, 3072], P(('groups', 'seq')), parts along dimension 0, may hold values from 0.01 to 1
Outputs:
- new_adapters: float32 [32, 4, 64, 3072], P(('groups', 'seq')), parts along dimension 0
- new_first: float32 [32, 4, 64, 3072], P(('groups', 'seq')), parts along dimension 0
- new_second: float32 [32, 4, 64, 3072], P(('groups', 'seq')), parts along dimension 0
The draws below stay inside these ranges and needn't reach their ends.
There are 2 independent parts, one for each index of `groups`. The reference program is written for one: setup_inputs(seed, part) draws one part's arguments, and reference() takes and returns one part's arrays. A program takes and returns all parts, laid end to end along the dimension named above; each array names one. Nothing has to cross between parts.
All inputs are finite; a program needn't handle non-finite values.
Results may differ from the reference program's by a relative error of at most 0.0022.
Values may be sent and summed in bfloat16 or wider, within the bound.
No kernel may reach another device: no remote copies, remote signals or barrier semaphores. Data moves between devices by JAX's collectives and lax.ppermute only.
A program may use at most 128 MiB of HBM per device.

```python
import math
import jax
import jax.numpy as jnp
import numpy as np
from jax import lax

HEADS = 24
HD = 128
D = 3072
R = 64
IMAGES = 4
L = 1024
TENANTS = 16


def set_ends(values, rng, smallest, largest):
    dims = values.shape
    index_at = [jax.random.randint(jax.random.fold_in(rng, axis), (), 0, dims[axis]) for axis in range(len(dims))]
    values = values.at[tuple(index_at)].set(smallest)
    longest = dims.index(max(dims))
    index_at[longest] = (index_at[longest] + 1) % dims[longest]
    return values.at[tuple(index_at)].set(largest)


def strengthened(array, own_key, source, target, blocks, factor):
    owner, partner = [(jnp.arange(array.shape[dim]) // (array.shape[dim] // blocks)).reshape([-1 if axis == dim else 1 for axis in range(array.ndim)]) for dim in (source, target)]
    chosen = jax.random.permutation(own_key, blocks)[partner]
    strong = (owner == chosen) | (owner == (partner + blocks // 2) % blocks)
    return jnp.where(strong, factor * array, array)


def steps_of(rng, dims, pieces, least, largest):
    def one(position, blocks):
        steps = jax.random.uniform(jax.random.fold_in(jax.random.fold_in(rng, 6), position), (blocks,), jnp.float32, least / len(pieces), largest / len(pieces))
        return jnp.repeat(jnp.exp(steps), dims[position] // blocks).reshape((-1,) + (1,) * (len(dims) - position - 1))

    loudness = one(*pieces[0])
    for cut in pieces[1:]:
        loudness = loudness * one(*cut)
    return loudness


def rank_table(number_of, slope):
    weights = [(1 << 20) // math.isqrt(rank ** slope) + 1 for rank in range(1, number_of + 1)]
    width = 1 + sum(weights) // (1 << 30)
    return np.cumsum(np.array([max(1, weight // width) for weight in weights]))


def ranked(key, dims, amount, lean):
    listing = rank_table(amount, lean)
    pick = jax.random.randint(jax.random.fold_in(key, 1), dims, 0, int(listing[amount - 1]))
    rank = jnp.searchsorted(jnp.asarray(listing, jnp.int32), pick, side="right")
    return jax.random.permutation(jax.random.fold_in(key, 2), amount)[rank].astype(jnp.int32)


def noise(key, dims, spread, bound, split=(), kind=jnp.bfloat16):
    level = steps_of(key, dims, split, -0.22, 0.18) if split else 1.0
    entries = jax.random.normal(key, dims, jnp.float32) * spread * level
    return jnp.minimum(jnp.maximum(entries, -bound), bound).astype(kind)


def heavy_noise(stream_key, dims, spread, limit, pieces, heavy, held_as=jnp.bfloat16):
    drawn = spread * jax.random.normal(stream_key, dims, jnp.float32)
    if pieces:
        drawn = drawn * steps_of(stream_key, dims, pieces, -0.22, 0.18)
    return jnp.clip(strengthened(drawn, jax.random.fold_in(stream_key, 3), *heavy), -limit, limit).astype(held_as)


def setup_inputs(seed: int = 0, part: int = 0) -> dict:
    key_of = jax.random.split(jax.random.key(seed), 12)
    own_keys = jax.random.split(jax.random.fold_in(key_of[11], part), 12)
    return {
        "tenant_ids": set_ends(ranked(own_keys[0], (IMAGES,), TENANTS, 2), jax.random.fold_in(own_keys[0], 3), 0, TENANTS - 1).astype(jnp.int32),
        "timesteps": set_ends(jax.random.randint(own_keys[1], (IMAGES,), 0, 1000), jax.random.fold_in(own_keys[1], 1), 0, 999).astype(jnp.int32),
        "counts": set_ends(jax.random.randint(own_keys[2], (TENANTS,), 1, 17), jax.random.fold_in(own_keys[2], 1), 1, 16).astype(jnp.int32),
        "hidden_in": heavy_noise(own_keys[3], (IMAGES, L, D), 1.0, 6.0, ((1, 16),), (1, 2, 16, 2.0)),
        "frozen_query": noise(own_keys[4], (IMAGES, L, D), 1.0, 6.0, ((1, 16),)),
        "key_base": noise(own_keys[5], (IMAGES, L, D), 1.0, 6.0, ((1, 16),)),
        "frozen_value": noise(own_keys[6], (IMAGES, L, D), 1.0, 6.0, ((1, 16),)),
        "out_grad": noise(own_keys[7], (IMAGES, L, D), 1.0, 6.0, ((1, 16),)),
        "adapters": noise(own_keys[8], (TENANTS, 4, R, D), 0.045, 0.625, ((0, 16),), jnp.float32),
        "first_moment": noise(own_keys[9], (TENANTS, 4, R, D), 0.3, 4.0, ((0, 16),), jnp.float32),
        "second_moment": jnp.clip(jnp.exp(math.log(1.0) - 4.6051702 * jax.random.uniform(own_keys[10], (TENANTS, 4, R, D), jnp.float32) ** steps_of(own_keys[10], (TENANTS, 4, R, D), ((0, 16),), -0.2, 0.2)), 0.01, 1.0),
    }


adapter_scale = 0.5
norm_eps = 1e-06
beta_one = 0.9
beta_two = 0.999
adam_eps = 1e-08
learn_rate = 0.01
adam_step = 100.0
num_steps = 1000.0

def head_norm(field_in):
    shaped = field_in.reshape(field_in.shape[:-1] + (HEADS, HD))
    inverse = lax.rsqrt(lax.optimization_barrier(jnp.mean(shaped * shaped, axis=-1, keepdims=True)) + norm_eps)
    return (shaped * inverse, inverse)

def pair_grads(query_n, key_n, value_rows, upstream):
    score_scale = HD ** (-0.5)
    scores = jnp.dot(query_n, key_n.T, preferred_element_type=jnp.float32) * score_scale
    exp_scores = jnp.exp(scores)
    attn_probs = exp_scores / lax.optimization_barrier(jnp.sum(exp_scores, axis=-1, keepdims=True))
    probs_b = attn_probs.astype(jnp.bfloat16)
    attn_out = jnp.dot(probs_b, value_rows, preferred_element_type=jnp.float32)
    row_delta = lax.optimization_barrier(jnp.sum(upstream.astype(jnp.float32) * attn_out, axis=-1, keepdims=True))
    dprobs = jnp.dot(upstream, value_rows.T, preferred_element_type=jnp.float32)
    dscores = (attn_probs * (dprobs - row_delta)).astype(jnp.bfloat16)
    dquery_n = (jnp.dot(dscores, key_n, preferred_element_type=jnp.float32) * score_scale).astype(jnp.bfloat16)
    value_gradient = jnp.dot(probs_b.T, upstream, preferred_element_type=jnp.float32).astype(jnp.bfloat16)
    return (dquery_n, value_gradient)

def split_heads(tokens_major):
    return tokens_major.reshape(L, HEADS, HD).transpose(1, 0, 2)

def join_heads(heads_major):
    return heads_major.transpose(1, 0, 2).reshape(L, D)

def reference(tenant_ids, timesteps, counts, hidden_in, frozen_query, key_base, frozen_value, out_grad, adapters, first_moment, second_moment):
    position_list = []
    for picture_index in range(IMAGES):
        tenant = tenant_ids[picture_index]
        loaded_adapters = lax.dynamic_index_in_dim(adapters, tenant, 0, keepdims=False).astype(jnp.bfloat16)
        input_items = hidden_in[picture_index]
        query_down_product = jnp.dot(input_items, loaded_adapters[0].T, preferred_element_type=jnp.float32).astype(jnp.bfloat16)
        value_down_product = jnp.dot(input_items, loaded_adapters[2].T, preferred_element_type=jnp.float32).astype(jnp.bfloat16)
        query_unscaled = frozen_query[picture_index].astype(jnp.float32) + adapter_scale * jnp.dot(query_down_product, loaded_adapters[1], preferred_element_type=jnp.float32)
        normed, inverse = head_norm(query_unscaled)
        query_n = normed.reshape(L, D).astype(jnp.bfloat16)
        key_normed, key_inverse = head_norm(key_base[picture_index].astype(jnp.float32))
        key_n = key_normed.reshape(L, D).astype(jnp.bfloat16)
        value_complete = (frozen_value[picture_index].astype(jnp.float32) + adapter_scale * jnp.dot(value_down_product, loaded_adapters[3], preferred_element_type=jnp.float32)).astype(jnp.bfloat16)
        weight_t = 1.0 / (((timesteps[picture_index].astype(jnp.float32) + 1.0) / num_steps) ** 2 + 0.25)
        upstream = (weight_t * out_grad[picture_index].astype(jnp.float32)).astype(jnp.bfloat16)
        dquery_heads, dvalue_heads = lax.map(lambda operands: pair_grads(*operands), (split_heads(query_n), split_heads(key_n), split_heads(value_complete), split_heads(upstream)))
        dquery_f = join_heads(dquery_heads).astype(jnp.float32).reshape(L, HEADS, HD)
        value_gradient = join_heads(dvalue_heads)
        query_gradient = (inverse * (dquery_f - normed * lax.optimization_barrier(jnp.mean(dquery_f * normed, axis=-1, keepdims=True)))).reshape(L, D).astype(jnp.bfloat16)
        query_gradient_rows = jnp.dot(query_gradient, loaded_adapters[1].T, preferred_element_type=jnp.float32).astype(jnp.bfloat16)
        value_gradient_rows = jnp.dot(value_gradient, loaded_adapters[3].T, preferred_element_type=jnp.float32).astype(jnp.bfloat16)
        position_list.append(jnp.stack([adapter_scale * jnp.dot(query_gradient_rows.T, input_items, preferred_element_type=jnp.float32), adapter_scale * jnp.dot(query_down_product.T, query_gradient, preferred_element_type=jnp.float32), adapter_scale * jnp.dot(value_gradient_rows.T, input_items, preferred_element_type=jnp.float32), adapter_scale * jnp.dot(value_down_product.T, value_gradient, preferred_element_type=jnp.float32)]))
    slots = jnp.stack(position_list)
    owners = (tenant_ids[None, :] == jnp.arange(TENANTS, dtype=jnp.int32)[:, None]).astype(jnp.float32)
    tenant_grad = jnp.einsum('ti,iabc->tabc', owners, slots, precision=lax.Precision.HIGHEST) / counts.astype(jnp.float32)[:, None, None, None]
    new_first = beta_one * first_moment + (1.0 - beta_one) * tenant_grad
    new_second = beta_two * second_moment + (1.0 - beta_two) * tenant_grad * tenant_grad
    first_corr = 1.0 - beta_one ** adam_step
    second_corr = 1.0 - beta_two ** adam_step
    new_adapters = adapters - learn_rate * (new_first / first_corr) / (jnp.sqrt(new_second / second_corr) + adam_eps)
    return (new_adapters, new_first, new_second)
```

```python
import functools
import math

import jax
import jax.numpy as jnp
from jax import lax
from jax.experimental import pallas as pl
from jax.experimental.pallas import tpu as pltpu
from jax.sharding import PartitionSpec as P

HEADS = 24
HD = 128
RANK = 64

adapter_scale = 0.5
norm_eps = 1e-06
beta_one = 0.9
beta_two = 0.999
adam_eps = 1e-08
learn_rate = 0.01
adam_step = 100.0
num_steps = 1000.0

SCORE_SCALE = HD ** (-0.5)
EXP_SCALE = SCORE_SCALE * math.log2(math.e)
VMEM_LIMIT = 50 << 20

MATS = (0, 2, 1, 3)

F32 = jnp.float32
BF16 = jnp.bfloat16


def dot(left, right):
    return jnp.dot(left, right, preferred_element_type=F32)


def dot_nt(left, right):
    return lax.dot_general(left, right, (((1,), (1,)), ((), ())), preferred_element_type=F32)


def dot_tn(left, right):
    return lax.dot_general(left, right, (((0,), (0,)), ((), ())), preferred_element_type=F32)


def exchange(block, flip, size):
    return lax.ppermute(block, "seq", [(i, i ^ flip) for i in range(size)])


def pack_kernel(chunks, weight_ref, query_ref, key_ref, value_ref, grad_ref, *out_refs):
    weight = weight_ref[pl.program_id(0)]
    head = 0
    for out_ref, count in zip(out_refs, chunks):
        for slot in range(count):
            cols = slice(head * HD, (head + 1) * HD)
            base = slot * 4 * HD
            key = key_ref[0, :, cols].astype(F32)
            inverse = lax.rsqrt(jnp.mean(key * key, axis=-1, keepdims=True) + norm_eps)
            out_ref[0, :, base : base + HD] = query_ref[0, :, cols]
            out_ref[0, :, base + HD : base + 2 * HD] = (key * inverse).astype(BF16)
            out_ref[0, :, base + 2 * HD : base + 3 * HD] = value_ref[0, :, cols]
            out_ref[0, :, base + 3 * HD : base + 4 * HD] = (
                weight * grad_ref[0, :, cols].astype(F32)
            ).astype(BF16)
            head += 1


def pack(weight_t, frozen_query, key_base, frozen_value, out_grad, per, chunks):
    images, rows, width = frozen_query.shape
    cols = width // per
    spec = pl.BlockSpec((1, rows, cols), lambda i, a: (i, 0, a))
    return pl.pallas_call(
        functools.partial(pack_kernel, chunks),
        grid=(images, per),
        in_specs=[pl.BlockSpec(memory_space=pltpu.SMEM)] + [spec] * 4,
        out_specs=[
            pl.BlockSpec((1, rows, n * 4 * HD), lambda i, a: (i * per + a, 0, 0)) for n in chunks
        ],
        out_shape=[jax.ShapeDtypeStruct((images * per, rows, n * 4 * HD), BF16) for n in chunks],
        compiler_params=pltpu.CompilerParams(vmem_limit_bytes=VMEM_LIMIT),
        cost_estimate=pl.CostEstimate(
            flops=0, bytes_accessed=16 * images * rows * width, transcendentals=0
        ),
        name="pack",
    )(weight_t, frozen_query, key_base, frozen_value, out_grad)


def attend_kernel(
    first, row_block, buf_ref, u_ref, bq_ref, bv_ref, *rest
):
    if first:
        gin_ref = None
    else:
        gin_ref, rest = rest[0], rest[1:]
    gout_ref, slot_ref, query_s, value_s, normed_s, inverse_s, dquery_s, dvalue_s, keyt_s = rest
    length = buf_ref.shape[0]

    @pl.when(pl.program_id(0) == 0)
    def _():
        gout_ref[...] = jnp.zeros_like(gout_ref) if first else gin_ref[...]

    query_raw = buf_ref[:, :HD].astype(F32) + adapter_scale * dot(u_ref[:, :RANK], bq_ref[...])
    inverse = lax.rsqrt(jnp.mean(query_raw * query_raw, axis=-1, keepdims=True) + norm_eps)
    normed = query_raw * inverse
    normed_s[...] = normed
    inverse_s[...] = jnp.broadcast_to(inverse, (length, HD))
    query_s[...] = normed.astype(BF16)
    value_s[...] = (
        buf_ref[:, 2 * HD : 3 * HD].astype(F32)
        + adapter_scale * dot(u_ref[:, RANK:], bv_ref[...])
    ).astype(BF16)
    key = buf_ref[:, HD : 2 * HD]
    keyt_s[...] = key.T
    for block in range(length // row_block):
        rows = slice(block * row_block, (block + 1) * row_block)
        upstream = buf_ref[rows, 3 * HD :]
        scores = dot_nt(key, query_s[rows, :])
        exp_scores = jnp.exp2(scores * EXP_SCALE)
        probs = exp_scores * (1.0 / jnp.sum(exp_scores, axis=0, keepdims=True))
        probs_b = probs.astype(BF16)
        dprobs = dot_nt(value_s[...], upstream)
        delta = jnp.sum(probs_b.astype(F32) * dprobs, axis=0, keepdims=True)
        dscores = (probs * (dprobs - delta)).astype(BF16)
        dquery_s[rows, :] = (dot(keyt_s[...], dscores) * SCORE_SCALE).T
        part = dot(probs_b, upstream)
        if block == 0:
            dvalue_s[...] = part
        else:
            dvalue_s[...] += part
    dquery_n = dquery_s[...].astype(BF16).astype(F32)
    normed = normed_s[...]
    dquery = (
        inverse_s[...]
        * (dquery_n - normed * jnp.mean(dquery_n * normed, axis=-1, keepdims=True))
    ).astype(BF16)
    dvalue = dvalue_s[...].astype(BF16)
    gout_ref[:, :RANK] += dot_nt(dquery, bq_ref[...])
    gout_ref[:, RANK:] += dot_nt(dvalue, bv_ref[...])
    slot_ref[:RANK, :] = (adapter_scale * dot_tn(u_ref[:, :RANK], dquery)).astype(slot_ref.dtype)
    slot_ref[RANK:, :] = (adapter_scale * dot_tn(u_ref[:, RANK:], dvalue)).astype(slot_ref.dtype)


def attend(received, u_rows, b_rows, partial_rows, first_head, send_type):
    length = received.shape[0]
    count = received.shape[1] // (4 * HD)
    first = partial_rows is None
    row_block = min(512, length)
    whole = lambda h: (0, 0)
    in_specs = [
        pl.BlockSpec((length, 4 * HD), lambda h: (0, h)),
        pl.BlockSpec((length, 2 * RANK), whole),
        pl.BlockSpec((RANK, HD), lambda h: (0, first_head + h)),
        pl.BlockSpec((RANK, HD), lambda h: (1, first_head + h)),
    ]
    operands = [received, u_rows, b_rows, b_rows]
    if not first:
        in_specs.append(pl.BlockSpec((length, 2 * RANK), whole))
        operands.append(partial_rows)
    return pl.pallas_call(
        functools.partial(attend_kernel, first, row_block),
        grid=(count,),
        in_specs=in_specs,
        out_specs=[
            pl.BlockSpec((length, 2 * RANK), whole),
            pl.BlockSpec((2 * RANK, HD), lambda h: (0, h)),
        ],
        out_shape=[
            jax.ShapeDtypeStruct((length, 2 * RANK), F32),
            jax.ShapeDtypeStruct((2 * RANK, count * HD), send_type),
        ],
        scratch_shapes=[
            pltpu.VMEM((length, HD), BF16),
            pltpu.VMEM((length, HD), BF16),
            pltpu.VMEM((length, HD), F32),
            pltpu.VMEM((length, HD), F32),
            pltpu.VMEM((length, HD), F32),
            pltpu.VMEM((length, HD), F32),
            pltpu.VMEM((HD, length), BF16),
        ],
        compiler_params=pltpu.CompilerParams(vmem_limit_bytes=VMEM_LIMIT),
        cost_estimate=pl.CostEstimate(
            flops=count * length * length * 10000,
            bytes_accessed=2 * received.size,
            transcendentals=count * length * length,
        ),
        name="attend",
    )(*operands)


def adam_kernel(per, where_ref, count_ref, *refs):
    grad_refs = refs[:per]
    adapter_ref, first_ref, second_ref, new_adapter_ref, new_first_ref, new_second_ref = refs[per:]
    first_corr = 1.0 - beta_one**adam_step
    second_corr = 1.0 - beta_two**adam_step
    divisor = count_ref[0].astype(F32)
    for m, grad_ref in enumerate(grad_refs):

        @pl.when(pl.program_id(0) == m)
        def _(grad_ref=grad_ref):
            for place, mat in enumerate(MATS):
                grad = grad_ref[place * RANK : (place + 1) * RANK, :].astype(F32) / divisor
                new_first = beta_one * first_ref[0, mat] + (1.0 - beta_one) * grad
                new_second = beta_two * second_ref[0, mat] + (1.0 - beta_two) * grad * grad
                new_first_ref[0, mat] = new_first
                new_second_ref[0, mat] = new_second
                new_adapter_ref[0, mat] = adapter_ref[0, mat] - learn_rate * (
                    new_first / first_corr
                ) / (jnp.sqrt(new_second / second_corr) + adam_eps)


def adam(place, counts, grads, adapters, first_moment, second_moment):
    per = len(grads)
    rows, cols = grads[0].shape
    state = pl.BlockSpec(
        (1, 4, RANK, cols), lambda m, where_ref, count_ref: (0, 0, 0, jnp.bitwise_xor(m, where_ref[0]))
    )
    grad = pl.BlockSpec((rows, cols), lambda m, where_ref, count_ref: (0, 0))
    return pl.pallas_call(
        functools.partial(adam_kernel, per),
        grid_spec=pltpu.PrefetchScalarGridSpec(
            num_scalar_prefetch=2,
            grid=(per,),
            in_specs=[grad] * per + [state] * 3,
            out_specs=[state] * 3,
        ),
        out_shape=[jax.ShapeDtypeStruct(adapters.shape, F32)] * 3,
        compiler_params=pltpu.CompilerParams(vmem_limit_bytes=VMEM_LIMIT),
        cost_estimate=pl.CostEstimate(
            flops=0, bytes_accessed=24 * adapters.size, transcendentals=0
        ),
        name="adam",
    )(place, counts, *grads, adapters, first_moment, second_moment)


def sum_rows(partial, place, per, size):
    length, width = partial.shape
    kept = partial.reshape((2,) * (per.bit_length() - 1) + (length // per, width))
    bits = per.bit_length() - 1
    for bit in range(bits):
        axis = bits - 1 - bit
        low = lax.index_in_dim(kept, 0, axis, keepdims=False)
        high = lax.index_in_dim(kept, 1, axis, keepdims=False)
        mine = ((place >> bit) & 1) == 1
        sent = jnp.where(mine, low, high)
        kept = jnp.where(mine, high, low) + exchange(sent, 1 << bit, size)
    rows = kept.astype(BF16)
    for bit in reversed(range(bits)):
        axis = bits - 1 - bit
        other = exchange(rows, 1 << bit, size)
        mine = ((place >> bit) & 1) == 1
        rows = jnp.stack(
            [jnp.where(mine, other, rows), jnp.where(mine, rows, other)], axis=axis
        )
    return rows.reshape(length, width)


def fetch_adapter(tenant_ids, adapters, zone, place, per, images, size):
    width = adapters.shape[-1]
    cols = width // per
    own = adapters[0]
    pieces = []
    for m in range(per):
        piece = lax.dynamic_slice_in_dim(own, (place ^ m) * cols, cols, axis=2)
        piece = jnp.stack([piece[mat] for mat in MATS]).reshape(4 * RANK, cols).astype(BF16)
        pieces.append(piece if m == 0 else exchange(piece, m, size))
    blocks = []
    for r in range(images):
        tenant = lax.dynamic_index_in_dim(tenant_ids, zone ^ r, 0, keepdims=False)
        block = jnp.zeros_like(pieces[0])
        for m, piece in enumerate(pieces):
            block = jnp.where(tenant == zone * per + (place ^ m), piece, block)
        blocks.append(block)
    bit = 1
    while len(blocks) > 1:
        sent = jnp.stack(blocks[1::2])
        came = exchange(sent, bit * per, size)
        blocks = [block + came[i] for i, block in enumerate(blocks[0::2])]
        bit *= 2
    return blocks[0]


def gather_images(slots, per, images, size):
    blocks = {0: slots}
    bit = images // 2
    while bit:
        known = sorted(blocks)
        came = exchange(jnp.stack([blocks[r] for r in known]), bit * per, size)
        for i, r in enumerate(known):
            blocks[r ^ bit] = came[i]
        bit //= 2
    return [blocks[r] for r in range(images)]


def shards(
    tenant_ids,
    timesteps,
    counts,
    hidden_in,
    frozen_query,
    key_base,
    frozen_value,
    out_grad,
    adapters,
    first_moment,
    second_moment,
):
    images, rows, width = hidden_in.shape
    size = lax.axis_size("seq")
    per = size // images
    cols = width // per
    heads = HEADS // per
    length = size * rows
    me = lax.axis_index("seq")
    zone, place = me // per, me % per
    chunks = (1,) * heads
    send_type = BF16

    hidden_sent = (
        hidden_in.reshape(images, rows, per, cols).transpose(0, 2, 1, 3).reshape(size, rows, cols)
    )
    hidden = lax.all_to_all(hidden_sent, "seq", 0, 0, tiled=True).reshape(length, cols)

    weight_t = 1.0 / (((timesteps.astype(F32) + 1.0) / num_steps) ** 2 + 0.25)
    packed = pack(weight_t, frozen_query, key_base, frozen_value, out_grad, per, chunks)

    adapter = fetch_adapter(tenant_ids, adapters, zone, place, per, images, size)
    a_rows, b_rows = adapter[: 2 * RANK], adapter[2 * RANK :]
    u_rows = sum_rows(dot_nt(hidden, a_rows), place, per, size)

    history = []
    partial_rows = None
    slots_b = []
    head = 0
    for step, count in enumerate(chunks):
        sent = packed[step]
        if step >= 2:
            sent, history[step - 2] = lax.optimization_barrier((sent, history[step - 2]))
        received = lax.all_to_all(sent, "seq", 0, 0, tiled=True).reshape(length, count * 4 * HD)
        if step >= 2:
            partial_rows = history[step - 1]
        elif step == 1:
            partial_rows = history[0]
        partial_rows, slot = attend(received, u_rows, b_rows, partial_rows, head, send_type)
        history.append(partial_rows)
        slots_b.append(slot)
        head += count

    grad_rows = sum_rows(partial_rows, place, per, size)
    slots_a = (adapter_scale * dot_tn(grad_rows, hidden)).astype(send_type)
    slots = jnp.concatenate([slots_a, jnp.concatenate(slots_b, axis=1)], axis=0)
    gathered = gather_images(slots, per, images, size)
    grads = []
    for m in range(per):
        tenant = zone * per + (place ^ m)
        total = jnp.zeros(slots.shape, F32)
        for r in range(images):
            owner = lax.dynamic_index_in_dim(tenant_ids, zone ^ r, 0, keepdims=False)
            total = total + jnp.where(owner == tenant, gathered[r].astype(F32), 0.0)
        total = total.astype(send_type)
        grads.append(total if m == 0 else exchange(total, m, size))
    return tuple(
        adam(place.reshape(1), counts, grads, adapters, first_moment, second_moment)
    )


def solution(mesh):
    whole = P(("groups", "seq"), None, None, None)
    tokens = P("groups", "seq", None)
    in_specs = (P("groups"), P("groups"), P(("groups", "seq"))) + (tokens,) * 5 + (whole,) * 3
    return jax.shard_map(
        shards, mesh=mesh, in_specs=in_specs, out_specs=(whole,) * 3, check_vma=False
    )
```

```python
import functools
import math

import jax
import jax.numpy as jnp
from jax import lax
from jax.experimental import pallas as pl
from jax.experimental.pallas import tpu as pltpu
from jax.sharding import PartitionSpec as P

HEADS = 24
HD = 128
RANK = 64

adapter_scale = 0.5
norm_eps = 1e-06
beta_one = 0.9
beta_two = 0.999
adam_eps = 1e-08
learn_rate = 0.01
adam_step = 100.0
num_steps = 1000.0

SCORE_SCALE = HD ** (-0.5)
EXP_SCALE = SCORE_SCALE * math.log2(math.e)
VMEM_LIMIT = 24 << 20

F32 = jnp.float32
BF16 = jnp.bfloat16


def dot(left, right):
    return jnp.dot(left, right, preferred_element_type=F32)


def dot_nt(left, right):
    return lax.dot_general(left, right, (((1,), (1,)), ((), ())), preferred_element_type=F32)


def dot_tn(left, right):
    return lax.dot_general(left, right, (((0,), (0,)), ((), ())), preferred_element_type=F32)


def exchange(block, flip, size):
    return lax.ppermute(block, "seq", [(i, i ^ flip) for i in range(size)])


def pack_kernel(chunks, per, steps_ref, query_ref, key_ref, value_ref, grad_ref, *out_refs):
    step = jnp.full((query_ref.shape[1], HD), steps_ref[pl.program_id(0)], jnp.int32)
    weight = 1.0 / (((step.astype(F32) + 1.0) / num_steps) ** 2 + 0.25)
    head = 0
    for dest in range(per):
        for out_ref, count in zip(out_refs, chunks):
            for slot in range(count):
                cols = slice(head * HD, (head + 1) * HD)
                base = slot * 4 * HD
                key = key_ref[0, :, cols].astype(F32)
                inverse = lax.rsqrt(jnp.mean(key * key, axis=-1, keepdims=True) + norm_eps)
                out_ref[dest, :, base : base + HD] = query_ref[0, :, cols]
                out_ref[dest, :, base + HD : base + 2 * HD] = (key * inverse).astype(BF16)
                out_ref[dest, :, base + 2 * HD : base + 3 * HD] = value_ref[0, :, cols]
                out_ref[dest, :, base + 3 * HD : base + 4 * HD] = (
                    weight * grad_ref[0, :, cols].astype(F32)
                ).astype(BF16)
                head += 1


def pack(timesteps, frozen_query, key_base, frozen_value, out_grad, per, chunks):
    images, rows, width = frozen_query.shape
    spec = pl.BlockSpec((1, rows, width), lambda i: (i, 0, 0))
    return pl.pallas_call(
        functools.partial(pack_kernel, chunks, per),
        grid=(images,),
        in_specs=[pl.BlockSpec(memory_space=pltpu.SMEM)] + [spec] * 4,
        out_specs=[pl.BlockSpec((per, rows, n * 4 * HD), lambda i: (i, 0, 0)) for n in chunks],
        out_shape=[jax.ShapeDtypeStruct((images * per, rows, n * 4 * HD), BF16) for n in chunks],
        compiler_params=pltpu.CompilerParams(vmem_limit_bytes=50 << 20),
        cost_estimate=pl.CostEstimate(
            flops=0, bytes_accessed=16 * images * rows * width, transcendentals=0
        ),
        name="pack",
    )(timesteps, frozen_query, key_base, frozen_value, out_grad)


def attend_kernel(
    first, row_block, buf_ref, u_ref, bq_ref, bv_ref, *rest
):
    if first:
        gin_ref = None
    else:
        gin_ref, rest = rest[0], rest[1:]
    gout_ref, slot_ref, query_s, value_s, normed_s, inverse_s, dquery_s, dvalue_s, keyt_s = rest
    length = buf_ref.shape[0]

    @pl.when(pl.program_id(0) == 0)
    def _():
        gout_ref[...] = jnp.zeros_like(gout_ref) if first else gin_ref[...]

    query_raw = buf_ref[:, :HD].astype(F32) + adapter_scale * dot(u_ref[:, :RANK], bq_ref[...])
    inverse = lax.rsqrt(jnp.mean(query_raw * query_raw, axis=-1, keepdims=True) + norm_eps)
    normed = query_raw * inverse
    normed_s[...] = normed
    inverse_s[...] = jnp.broadcast_to(inverse, (length, HD))
    query_s[...] = normed.astype(BF16)
    value_s[...] = (
        buf_ref[:, 2 * HD : 3 * HD].astype(F32)
        + adapter_scale * dot(u_ref[:, RANK:], bv_ref[...])
    ).astype(BF16)
    key = buf_ref[:, HD : 2 * HD]
    keyt_s[...] = key.T
    for block in range(length // row_block):
        rows = slice(block * row_block, (block + 1) * row_block)
        upstream = buf_ref[rows, 3 * HD :]
        scores = dot_nt(key, query_s[rows, :])
        exp_scores = jnp.exp2(scores * EXP_SCALE)
        probs = exp_scores * (1.0 / jnp.sum(exp_scores, axis=0, keepdims=True))
        probs_b = probs.astype(BF16)
        dprobs = dot_nt(value_s[...], upstream)
        delta = jnp.sum(probs_b.astype(F32) * dprobs, axis=0, keepdims=True)
        dscores = (probs * (dprobs - delta)).astype(BF16)
        dquery_s[rows, :] = (dot(keyt_s[...], dscores) * SCORE_SCALE).T
        part = dot(probs_b, upstream)
        if block == 0:
            dvalue_s[...] = part
        else:
            dvalue_s[...] += part
    dquery_n = dquery_s[...].astype(BF16).astype(F32)
    normed = normed_s[...]
    dquery = (
        inverse_s[...]
        * (dquery_n - normed * jnp.mean(dquery_n * normed, axis=-1, keepdims=True))
    ).astype(BF16)
    dvalue = dvalue_s[...].astype(BF16)
    gout_ref[:, :RANK] += dot_nt(dquery, bq_ref[...])
    gout_ref[:, RANK:] += dot_nt(dvalue, bv_ref[...])
    slot_ref[:RANK, :] = (adapter_scale * dot_tn(u_ref[:, :RANK], dquery)).astype(slot_ref.dtype)
    slot_ref[RANK:, :] = (adapter_scale * dot_tn(u_ref[:, RANK:], dvalue)).astype(slot_ref.dtype)


def attend(received, u_rows, b_rows, partial_rows, first_head, send_type):
    length = received.shape[0]
    count = received.shape[1] // (4 * HD)
    first = partial_rows is None
    row_block = min(512, length)
    whole = lambda h: (0, 0)
    in_specs = [
        pl.BlockSpec((length, 4 * HD), lambda h: (0, h)),
        pl.BlockSpec((length, 2 * RANK), whole),
        pl.BlockSpec((RANK, HD), lambda h: (0, first_head + h)),
        pl.BlockSpec((RANK, HD), lambda h: (1, first_head + h)),
    ]
    operands = [received, u_rows, b_rows, b_rows]
    if not first:
        in_specs.append(pl.BlockSpec((length, 2 * RANK), whole))
        operands.append(partial_rows)
    return pl.pallas_call(
        functools.partial(attend_kernel, first, row_block),
        grid=(count,),
        in_specs=in_specs,
        out_specs=[
            pl.BlockSpec((length, 2 * RANK), whole),
            pl.BlockSpec((2 * RANK, HD), lambda h: (0, h)),
        ],
        out_shape=[
            jax.ShapeDtypeStruct((length, 2 * RANK), F32),
            jax.ShapeDtypeStruct((2 * RANK, count * HD), send_type),
        ],
        scratch_shapes=[
            pltpu.VMEM((length, HD), BF16),
            pltpu.VMEM((length, HD), BF16),
            pltpu.VMEM((length, HD), F32),
            pltpu.VMEM((length, HD), F32),
            pltpu.VMEM((length, HD), F32),
            pltpu.VMEM((length, HD), F32),
            pltpu.VMEM((HD, length), BF16),
        ],
        compiler_params=pltpu.CompilerParams(vmem_limit_bytes=VMEM_LIMIT),
        cost_estimate=pl.CostEstimate(
            flops=count * length * length * 10000,
            bytes_accessed=2 * received.size,
            transcendentals=count * length * length,
        ),
        name="attend",
    )(*operands)


def adam_kernel(per, where_ref, count_ref, *refs):
    early_refs, late_refs, refs = refs[:per], refs[per : 2 * per], refs[2 * per :]
    adapter_ref, first_ref, second_ref, new_adapter_ref, new_first_ref, new_second_ref = refs
    cols = adapter_ref.shape[-1]
    early = early_refs[0].shape[-1]
    first_corr = 1.0 - beta_one**adam_step
    second_corr = 1.0 - beta_two**adam_step
    share = 1.0 / count_ref[0].astype(F32)

    def step(mat, where, grad):
        grad = grad.astype(F32) * share
        new_first = beta_one * first_ref[0, mat, :, where] + (1.0 - beta_one) * grad
        new_second = beta_two * second_ref[0, mat, :, where] + (1.0 - beta_two) * grad * grad
        new_first_ref[0, mat, :, where] = new_first
        new_second_ref[0, mat, :, where] = new_second
        corrected = new_second * (1.0 / second_corr)
        root = corrected * lax.rsqrt(corrected)
        new_adapter_ref[0, mat, :, where] = adapter_ref[0, mat, :, where] - (
            learn_rate / first_corr
        ) * new_first / (root + adam_eps)

    for m in range(per):

        @pl.when(pl.program_id(0) == m)
        def _(m=m):
            step(0, slice(0, cols), late_refs[m][:, :cols])
            step(1, slice(0, early), early_refs[m][...])
            step(1, slice(early, cols), late_refs[m][:, cols:])


def adam(place, counts, early, late, adapters, first_moment, second_moment):
    per = len(early)
    cols = adapters.shape[-1] // per
    state = pl.BlockSpec(
        (1, 2, RANK, cols),
        lambda m, p, where_ref, count_ref: (0, p, 0, jnp.bitwise_xor(m, where_ref[0])),
    )
    grads = [
        pl.BlockSpec((RANK, grad.shape[1]), lambda m, p, where_ref, count_ref: (p, 0))
        for grad in (*early, *late)
    ]
    return pl.pallas_call(
        functools.partial(adam_kernel, per),
        grid_spec=pltpu.PrefetchScalarGridSpec(
            num_scalar_prefetch=2,
            grid=(per, 2),
            in_specs=grads + [state] * 3,
            out_specs=[state] * 3,
        ),
        out_shape=[jax.ShapeDtypeStruct(adapters.shape, F32)] * 3,
        compiler_params=pltpu.CompilerParams(vmem_limit_bytes=VMEM_LIMIT),
        cost_estimate=pl.CostEstimate(
            flops=0, bytes_accessed=24 * adapters.size, transcendentals=0
        ),
        name="adam",
    )(place, counts, *early, *late, adapters, first_moment, second_moment)


def reduce_scatter_rows(partial, place, per, size):
    rows = partial.shape[0] // per
    total = lax.dynamic_slice_in_dim(partial, place * rows, rows, axis=0)
    came = [
        exchange(lax.dynamic_slice_in_dim(partial, (place ^ m) * rows, rows, axis=0), m, size)
        for m in range(1, per)
    ]
    for block in came:
        total = total + block
    return total.astype(BF16)


def gather_rows(total, per, size):
    return [total] + [exchange(total, m, size) for m in range(1, per)]


def in_order(blocks, place):
    bit = 1
    while bit < len(blocks):
        flip = (place & bit) != 0
        blocks = [
            jnp.where(flip, blocks[i ^ bit], blocks[i]) for i in range(len(blocks))
        ]
        bit *= 2
    return jnp.concatenate(blocks, axis=0)


def slot_kernel(per, where_ref, *refs):
    row_refs, (hidden_ref, last_ref, out_ref, total_s) = refs[:per], refs[per:]
    cols = hidden_ref.shape[1]
    for m, row_ref in enumerate(row_refs):

        @pl.when(pl.program_id(0) == m)
        def _(row_ref=row_ref, m=m):
            part = dot_tn(row_ref[...], hidden_ref[...])
            if m:
                part = part + total_s[...]
            if m < per - 1:
                total_s[...] = part
            else:
                out_ref[:, :cols] = (adapter_scale * part).astype(out_ref.dtype)
                out_ref[:, cols:] = last_ref[...]


def slots_of_hidden(place, blocks, hidden, last):
    per = len(blocks)
    rows, width = blocks[0].shape
    cols = hidden.shape[1]
    whole = lambda m, where_ref: (0, 0)
    return pl.pallas_call(
        functools.partial(slot_kernel, per),
        grid_spec=pltpu.PrefetchScalarGridSpec(
            num_scalar_prefetch=1,
            grid=(per,),
            in_specs=[pl.BlockSpec((rows, width), whole)] * per
            + [
                pl.BlockSpec((rows, cols), lambda m, where_ref: (jnp.bitwise_xor(m, where_ref[0]), 0)),
                pl.BlockSpec(last.shape, whole),
            ],
            out_specs=pl.BlockSpec((width, cols + last.shape[1]), whole),
            scratch_shapes=[pltpu.VMEM((width, cols), F32)],
        ),
        out_shape=jax.ShapeDtypeStruct((width, cols + last.shape[1]), last.dtype),
        compiler_params=pltpu.CompilerParams(vmem_limit_bytes=VMEM_LIMIT),
        cost_estimate=pl.CostEstimate(
            flops=2 * rows * per * width * cols, bytes_accessed=2 * hidden.size, transcendentals=0
        ),
        name="slots",
    )(place, *blocks, hidden, last)


def tie(values, *others):
    return lax.optimization_barrier((values, others))[0]


def pieces_kernel(per, where_ref, adapter_ref, *out_refs):
    for m in range(per):

        @pl.when(pl.program_id(0) == m)
        def _(m=m):
            for half in range(2):
                for row, mat in enumerate((half, half + 2)):
                    out_refs[half * per + m][row * RANK : (row + 1) * RANK, :] = adapter_ref[
                        0, mat
                    ].astype(BF16)


def column_pieces(place, adapters, per):
    cols = adapters.shape[-1] // per
    pieces = pl.pallas_call(
        functools.partial(pieces_kernel, per),
        grid_spec=pltpu.PrefetchScalarGridSpec(
            num_scalar_prefetch=1,
            grid=(per,),
            in_specs=[
                pl.BlockSpec(
                    (1, 4, RANK, cols),
                    lambda m, where_ref: (0, 0, 0, jnp.bitwise_xor(m, where_ref[0])),
                )
            ],
            out_specs=[pl.BlockSpec((2 * RANK, cols), lambda m, where_ref: (0, 0))] * (2 * per),
        ),
        out_shape=[jax.ShapeDtypeStruct((2 * RANK, cols), BF16)] * (2 * per),
        compiler_params=pltpu.CompilerParams(vmem_limit_bytes=VMEM_LIMIT),
        cost_estimate=pl.CostEstimate(
            flops=0, bytes_accessed=6 * adapters.size, transcendentals=0
        ),
        name="pieces",
    )(place, adapters)
    return pieces[:per], pieces[per:]


def spread(pieces, size):
    return [piece if m == 0 else exchange(piece, m, size) for m, piece in enumerate(pieces)]


def for_images_kernel(per, images, where_ref, ids_ref, *refs):
    piece_refs, (kept_ref, sent_ref) = refs[:per], refs[per:]
    zone, place = where_ref[0], where_ref[1]
    for r in range(images):
        tenant = ids_ref[jnp.bitwise_xor(zone, r)]
        block = jnp.zeros(piece_refs[0].shape, BF16)
        for m, piece_ref in enumerate(piece_refs):
            owner = zone * per + jnp.bitwise_xor(place, m)
            block = jnp.where(tenant == owner, piece_ref[...], block)
        if r % 2:
            sent_ref[r // 2] = block
        else:
            kept_ref[r // 2] = block


def for_images(where, tenant_ids, pieces):
    images = tenant_ids.shape[0]
    shape = (images // 2,) + pieces[0].shape
    smem = pl.BlockSpec(memory_space=pltpu.SMEM)
    return pl.pallas_call(
        functools.partial(for_images_kernel, len(pieces), images),
        in_specs=[smem, smem] + [pl.BlockSpec(memory_space=pltpu.VMEM)] * len(pieces),
        out_specs=[pl.BlockSpec(memory_space=pltpu.VMEM)] * 2,
        out_shape=[jax.ShapeDtypeStruct(shape, BF16)] * 2,
        compiler_params=pltpu.CompilerParams(vmem_limit_bytes=VMEM_LIMIT),
        cost_estimate=pl.CostEstimate(
            flops=0, bytes_accessed=8 * images * pieces[0].size, transcendentals=0
        ),
        name="for_images",
    )(where, tenant_ids, *pieces)


def halve_all(kept, came, per, size):
    blocks = [kept[i] + came[i] for i in range(kept.shape[0])]
    bit = 2
    while len(blocks) > 1:
        came = exchange(jnp.stack(blocks[1::2]), bit * per, size)
        blocks = [block + came[i] for i, block in enumerate(blocks[0::2])]
        bit *= 2
    return blocks[0]


def direct_images(slots, per, images, size):
    return [slots] + [exchange(slots, r * per, size) for r in range(1, images)]


def owner_kernel(per, images, where_ref, ids_ref, *refs):
    image_refs, sum_refs = refs[:images], refs[images:]
    zone, place = where_ref[0], where_ref[1]
    for m, sum_ref in enumerate(sum_refs):
        owner = zone * per + jnp.bitwise_xor(place, m)
        total = jnp.zeros(sum_ref.shape, F32)
        for r, image_ref in enumerate(image_refs):
            mine = ids_ref[jnp.bitwise_xor(zone, r)] == owner
            total = total + jnp.where(mine, image_ref[...].astype(F32), 0.0)
        sum_ref[...] = total.astype(sum_ref.dtype)


def owner_sums(where, tenant_ids, gathered, per, size):
    images = len(gathered)
    smem = pl.BlockSpec(memory_space=pltpu.SMEM)
    vmem = pl.BlockSpec(memory_space=pltpu.VMEM)
    sums = pl.pallas_call(
        functools.partial(owner_kernel, per, images),
        in_specs=[smem, smem] + [vmem] * images,
        out_specs=[vmem] * per,
        out_shape=[jax.ShapeDtypeStruct(gathered[0].shape, gathered[0].dtype)] * per,
        compiler_params=pltpu.CompilerParams(vmem_limit_bytes=VMEM_LIMIT),
        cost_estimate=pl.CostEstimate(
            flops=0, bytes_accessed=4 * images * gathered[0].size, transcendentals=0
        ),
        name="owner_sums",
    )(where, tenant_ids, *gathered)
    return [total if m == 0 else exchange(total, m, size) for m, total in enumerate(sums)]


def shards(
    tenant_ids,
    timesteps,
    counts,
    hidden_in,
    frozen_query,
    key_base,
    frozen_value,
    out_grad,
    adapters,
    first_moment,
    second_moment,
):
    images, rows, width = hidden_in.shape
    size = lax.axis_size("seq")
    per = size // images
    cols = width // per
    heads = HEADS // per
    length = size * rows
    me = lax.axis_index("seq")
    zone, place = me // per, me % per
    chunks = (heads - 1, 1)
    send_type = BF16

    hidden_sent = (
        hidden_in.reshape(images, rows, per, cols).transpose(0, 2, 1, 3).reshape(size, rows, cols)
    )
    pieces_a, pieces_b = column_pieces(place.reshape(1), adapters, per)
    pieces_a = spread(pieces_a, size)
    hidden_sent = tie(hidden_sent, pieces_a[1])
    hidden = lax.all_to_all(hidden_sent, "seq", 0, 0, tiled=True).reshape(length, cols)

    packed = pack(timesteps, frozen_query, key_base, frozen_value, out_grad, per, chunks)

    where = jnp.stack([zone, place])
    pieces_a = tie(pieces_a, packed)
    a_kept, a_sent = for_images(where, tenant_ids, pieces_a)
    a_came = exchange(a_sent, per, size)
    b_kept, b_sent = for_images(where, tenant_ids, spread(pieces_b, size))
    a_rows = halve_all(a_kept, a_came, per, size)
    b_rows = halve_all(b_kept, exchange(b_sent, per, size), per, size)

    packed = tie(packed, a_rows)
    u_total = reduce_scatter_rows(dot_nt(hidden, a_rows), place, per, size)

    u_rows = in_order(gather_rows(u_total, per, size), place)

    partial_rows = None
    head = 0
    slots_b = []
    for sent, count in zip(packed, chunks):
        received = lax.all_to_all(sent, "seq", 0, 0, tiled=True).reshape(length, count * 4 * HD)
        partial_rows, slot = attend(received, u_rows, b_rows, partial_rows, head, send_type)
        slots_b.append(slot)
        head += count
    early = {0: slots_b[0]}
    early[images // 2] = exchange(early[0], images // 2 * per, size)
    partial_rows = tie(partial_rows, early[images // 2])

    grad_total = reduce_scatter_rows(partial_rows, place, per, size)
    grad_rows = gather_rows(grad_total, per, size)
    bit = images // 4
    while bit:
        known = sorted(early)
        came = exchange(jnp.stack([early[r] for r in known]), bit * per, size)
        for i, r in enumerate(known):
            early[r ^ bit] = came[i]
        bit //= 2
    late = slots_of_hidden(place.reshape(1), grad_rows, hidden, slots_b[1])
    late = direct_images(late, per, images, size)
    early = owner_sums(where, tenant_ids, [early[r] for r in range(images)], per, size)
    late = [late[0]] + tie(late[1:], early)
    late = owner_sums(where, tenant_ids, late, per, size)
    return tuple(
        adam(place.reshape(1), counts, early, late, adapters, first_moment, second_moment)
    )


def solution(mesh):
    whole = P(("groups", "seq"), None, None, None)
    tokens = P("groups", "seq", None)
    in_specs = (P("groups"), P("groups"), P(("groups", "seq"))) + (tokens,) * 5 + (whole,) * 3
    return jax.shard_map(
        shards, mesh=mesh, in_specs=in_specs, out_specs=(whole,) * 3, check_vma=False
    )
```

```python
import functools
import math

import jax
import jax.numpy as jnp
from jax import lax
from jax.experimental import pallas as pl
from jax.experimental.pallas import tpu as pltpu
from jax.sharding import PartitionSpec as P

HEADS = 24
HD = 128
RANK = 64

adapter_scale = 0.5
norm_eps = 1e-06
beta_one = 0.9
beta_two = 0.999
adam_eps = 1e-08
learn_rate = 0.01
adam_step = 100.0
num_steps = 1000.0

SCORE_SCALE = HD ** (-0.5)
EXP_SCALE = SCORE_SCALE * math.log2(math.e)
VMEM_LIMIT = 24 << 20

F32 = jnp.float32
BF16 = jnp.bfloat16


def dot(left, right):
    return jnp.dot(left, right, preferred_element_type=F32)


def dot_nt(left, right):
    return lax.dot_general(left, right, (((1,), (1,)), ((), ())), preferred_element_type=F32)


def dot_tn(left, right):
    return lax.dot_general(left, right, (((0,), (0,)), ((), ())), preferred_element_type=F32)


def exchange(block, flip, size):
    return lax.ppermute(block, "seq", [(i, i ^ flip) for i in range(size)])


def pack_kernel(chunks, per, steps_ref, query_ref, key_ref, value_ref, grad_ref, *out_refs):
    step = jnp.full((query_ref.shape[1], HD), steps_ref[pl.program_id(0)], jnp.int32)
    weight = 1.0 / (((step.astype(F32) + 1.0) / num_steps) ** 2 + 0.25)
    head = 0
    for dest in range(per):
        for out_ref, count in zip(out_refs, chunks):
            for slot in range(count):
                cols = slice(head * HD, (head + 1) * HD)
                base = slot * 4 * HD
                key = key_ref[0, :, cols].astype(F32)
                inverse = lax.rsqrt(jnp.mean(key * key, axis=-1, keepdims=True) + norm_eps)
                out_ref[dest, :, base : base + HD] = query_ref[0, :, cols]
                out_ref[dest, :, base + HD : base + 2 * HD] = (key * inverse).astype(BF16)
                out_ref[dest, :, base + 2 * HD : base + 3 * HD] = value_ref[0, :, cols]
                out_ref[dest, :, base + 3 * HD : base + 4 * HD] = (
                    weight * grad_ref[0, :, cols].astype(F32)
                ).astype(BF16)
                head += 1


def pack(timesteps, frozen_query, key_base, frozen_value, out_grad, per, chunks):
    images, rows, width = frozen_query.shape
    spec = pl.BlockSpec((1, rows, width), lambda i: (i, 0, 0))
    return pl.pallas_call(
        functools.partial(pack_kernel, chunks, per),
        grid=(images,),
        in_specs=[pl.BlockSpec(memory_space=pltpu.SMEM)] + [spec] * 4,
        out_specs=[pl.BlockSpec((per, rows, n * 4 * HD), lambda i: (i, 0, 0)) for n in chunks],
        out_shape=[jax.ShapeDtypeStruct((images * per, rows, n * 4 * HD), BF16) for n in chunks],
        compiler_params=pltpu.CompilerParams(vmem_limit_bytes=50 << 20),
        cost_estimate=pl.CostEstimate(
            flops=0, bytes_accessed=16 * images * rows * width, transcendentals=0
        ),
        name="pack",
    )(timesteps, frozen_query, key_base, frozen_value, out_grad)


def attend_kernel(
    first, row_block, buf_ref, u_ref, bq_ref, bv_ref, *rest
):
    if first:
        gin_ref = None
    else:
        gin_ref, rest = rest[0], rest[1:]
    gout_ref, slot_ref, query_s, value_s, normed_s, inverse_s, dquery_s, dvalue_s, keyt_s = rest
    length = buf_ref.shape[0]

    @pl.when(pl.program_id(0) == 0)
    def _():
        gout_ref[...] = jnp.zeros_like(gout_ref) if first else gin_ref[...]

    query_raw = buf_ref[:, :HD].astype(F32) + adapter_scale * dot(u_ref[:, :RANK], bq_ref[...])
    inverse = lax.rsqrt(jnp.mean(query_raw * query_raw, axis=-1, keepdims=True) + norm_eps)
    normed = query_raw * inverse
    normed_s[...] = normed
    inverse_s[...] = jnp.broadcast_to(inverse, (length, HD))
    query_s[...] = normed.astype(BF16)
    value_s[...] = (
        buf_ref[:, 2 * HD : 3 * HD].astype(F32)
        + adapter_scale * dot(u_ref[:, RANK:], bv_ref[...])
    ).astype(BF16)
    key = buf_ref[:, HD : 2 * HD]
    keyt_s[...] = key.T
    for block in range(length // row_block):
        rows = slice(block * row_block, (block + 1) * row_block)
        upstream = buf_ref[rows, 3 * HD :]
        scores = dot_nt(key, query_s[rows, :])
        exp_scores = jnp.exp2(scores * EXP_SCALE)
        probs = exp_scores * (1.0 / jnp.sum(exp_scores, axis=0, keepdims=True))
        probs_b = probs.astype(BF16)
        dprobs = dot_nt(value_s[...], upstream)
        delta = jnp.sum(probs_b.astype(F32) * dprobs, axis=0, keepdims=True)
        dscores = (probs * (dprobs - delta)).astype(BF16)
        dquery_s[rows, :] = (dot(keyt_s[...], dscores) * SCORE_SCALE).T
        part = dot(probs_b, upstream)
        if block == 0:
            dvalue_s[...] = part
        else:
            dvalue_s[...] += part
    dquery_n = dquery_s[...].astype(BF16).astype(F32)
    normed = normed_s[...]
    dquery = (
        inverse_s[...]
        * (dquery_n - normed * jnp.mean(dquery_n * normed, axis=-1, keepdims=True))
    ).astype(BF16)
    dvalue = dvalue_s[...].astype(BF16)
    gout_ref[:, :RANK] += dot_nt(dquery, bq_ref[...])
    gout_ref[:, RANK:] += dot_nt(dvalue, bv_ref[...])
    slot_ref[:RANK, :] = (adapter_scale * dot_tn(u_ref[:, :RANK], dquery)).astype(slot_ref.dtype)
    slot_ref[RANK:, :] = (adapter_scale * dot_tn(u_ref[:, RANK:], dvalue)).astype(slot_ref.dtype)


def attend(received, u_rows, b_rows, partial_rows, first_head, send_type):
    length = received.shape[0]
    count = received.shape[1] // (4 * HD)
    first = partial_rows is None
    row_block = min(512, length)
    whole = lambda h: (0, 0)
    in_specs = [
        pl.BlockSpec((length, 4 * HD), lambda h: (0, h)),
        pl.BlockSpec((length, 2 * RANK), whole),
        pl.BlockSpec((RANK, HD), lambda h: (0, first_head + h)),
        pl.BlockSpec((RANK, HD), lambda h: (1, first_head + h)),
    ]
    operands = [received, u_rows, b_rows, b_rows]
    if not first:
        in_specs.append(pl.BlockSpec((length, 2 * RANK), whole))
        operands.append(partial_rows)
    return pl.pallas_call(
        functools.partial(attend_kernel, first, row_block),
        grid=(count,),
        in_specs=in_specs,
        out_specs=[
            pl.BlockSpec((length, 2 * RANK), whole),
            pl.BlockSpec((2 * RANK, HD), lambda h: (0, h)),
        ],
        out_shape=[
            jax.ShapeDtypeStruct((length, 2 * RANK), F32),
            jax.ShapeDtypeStruct((2 * RANK, count * HD), send_type),
        ],
        scratch_shapes=[
            pltpu.VMEM((length, HD), BF16),
            pltpu.VMEM((length, HD), BF16),
            pltpu.VMEM((length, HD), F32),
            pltpu.VMEM((length, HD), F32),
            pltpu.VMEM((length, HD), F32),
            pltpu.VMEM((length, HD), F32),
            pltpu.VMEM((HD, length), BF16),
        ],
        compiler_params=pltpu.CompilerParams(vmem_limit_bytes=VMEM_LIMIT),
        cost_estimate=pl.CostEstimate(
            flops=count * length * length * 10 * HD,
            bytes_accessed=2 * received.size,
            transcendentals=count * length * length,
        ),
        name="attend",
    )(*operands)


def adam_kernel(per, where_ref, count_ref, *refs):
    early_refs, late_refs, refs = refs[:per], refs[per : 2 * per], refs[2 * per :]
    adapter_ref, first_ref, second_ref, new_adapter_ref, new_first_ref, new_second_ref = refs
    first_corr = 1.0 - beta_one**adam_step
    second_corr = 1.0 - beta_two**adam_step
    share = 1.0 / count_ref[0].astype(F32)

    def step(mat, grad_ref):
        row = mat // 2 * RANK
        grad = grad_ref[row : row + RANK, :]
        grad = grad.astype(F32) * share
        new_first = beta_one * first_ref[0, mat] + (1.0 - beta_one) * grad
        new_second = beta_two * second_ref[0, mat] + (1.0 - beta_two) * grad * grad
        new_first_ref[0, mat] = new_first
        new_second_ref[0, mat] = new_second
        corrected = new_second * (1.0 / second_corr)
        root = corrected * lax.rsqrt(corrected)
        new_adapter_ref[0, mat] = adapter_ref[0, mat] - (learn_rate / first_corr) * new_first / (
            root + adam_eps
        )

    for m in range(per):

        @pl.when(pl.program_id(0) == m)
        def _(m=m):
            for half in range(2):
                step(2 * half, late_refs[m])
                step(2 * half + 1, early_refs[m])


def adam(place, counts, early, late, adapters, first_moment, second_moment):
    per = len(early)
    cols = adapters.shape[-1] // per
    state = pl.BlockSpec(
        (1, 4, RANK, cols),
        lambda m, where_ref, count_ref: (0, 0, 0, jnp.bitwise_xor(m, where_ref[0])),
    )
    grads = [
        pl.BlockSpec(grad.shape, lambda m, where_ref, count_ref: (0, 0))
        for grad in (*early, *late)
    ]
    return pl.pallas_call(
        functools.partial(adam_kernel, per),
        grid_spec=pltpu.PrefetchScalarGridSpec(
            num_scalar_prefetch=2,
            grid=(per,),
            in_specs=grads + [state] * 3,
            out_specs=[state] * 3,
        ),
        out_shape=[jax.ShapeDtypeStruct(adapters.shape, F32)] * 3,
        compiler_params=pltpu.CompilerParams(vmem_limit_bytes=VMEM_LIMIT),
        cost_estimate=pl.CostEstimate(
            flops=0, bytes_accessed=24 * adapters.size, transcendentals=0
        ),
        name="adam",
    )(place, counts, *early, *late, adapters, first_moment, second_moment)


def reduce_scatter_rows(partial, place, per, size):
    rows = partial.shape[0] // per
    total = lax.dynamic_slice_in_dim(partial, place * rows, rows, axis=0)
    came = [
        exchange(lax.dynamic_slice_in_dim(partial, (place ^ m) * rows, rows, axis=0), m, size)
        for m in range(1, per)
    ]
    for block in came:
        total = total + block
    return total.astype(BF16)


def gather_rows(total, per, size):
    return [total] + [exchange(total, m, size) for m in range(1, per)]


def in_order(blocks, place):
    bit = 1
    while bit < len(blocks):
        flip = (place & bit) != 0
        blocks = [
            jnp.where(flip, blocks[i ^ bit], blocks[i]) for i in range(len(blocks))
        ]
        bit *= 2
    return jnp.concatenate(blocks, axis=0)


def slot_kernel(per, where_ref, *refs):
    row_refs, (hidden_ref, out_ref, total_s) = refs[:per], refs[per:]
    for m, row_ref in enumerate(row_refs):

        @pl.when(pl.program_id(0) == m)
        def _(row_ref=row_ref, m=m):
            part = dot_tn(row_ref[...], hidden_ref[...])
            if m:
                part = part + total_s[...]
            if m < per - 1:
                total_s[...] = part
            else:
                out_ref[...] = (adapter_scale * part).astype(out_ref.dtype)


def slots_of_hidden(place, blocks, hidden, send_type):
    per = len(blocks)
    rows, width = blocks[0].shape
    cols = hidden.shape[1]
    whole = lambda m, where_ref: (0, 0)
    return pl.pallas_call(
        functools.partial(slot_kernel, per),
        grid_spec=pltpu.PrefetchScalarGridSpec(
            num_scalar_prefetch=1,
            grid=(per,),
            in_specs=[pl.BlockSpec((rows, width), whole)] * per
            + [pl.BlockSpec((rows, cols), lambda m, where_ref: (jnp.bitwise_xor(m, where_ref[0]), 0))],
            out_specs=pl.BlockSpec((width, cols), whole),
            scratch_shapes=[pltpu.VMEM((width, cols), F32)],
        ),
        out_shape=jax.ShapeDtypeStruct((width, cols), send_type),
        compiler_params=pltpu.CompilerParams(vmem_limit_bytes=VMEM_LIMIT),
        cost_estimate=pl.CostEstimate(
            flops=2 * rows * per * width * cols, bytes_accessed=2 * hidden.size, transcendentals=0
        ),
        name="slots",
    )(place, *blocks, hidden)


def tie(*values):
    return lax.optimization_barrier(values)


def pieces_kernel(per, where_ref, adapter_ref, *out_refs):
    for m in range(per):

        @pl.when(pl.program_id(0) == m)
        def _(m=m):
            for half in range(2):
                for row, mat in enumerate((half, half + 2)):
                    out_refs[half * per + m][row * RANK : (row + 1) * RANK, :] = adapter_ref[
                        0, mat
                    ].astype(BF16)


def column_pieces(place, adapters, per):
    cols = adapters.shape[-1] // per
    pieces = pl.pallas_call(
        functools.partial(pieces_kernel, per),
        grid_spec=pltpu.PrefetchScalarGridSpec(
            num_scalar_prefetch=1,
            grid=(per,),
            in_specs=[
                pl.BlockSpec(
                    (1, 4, RANK, cols),
                    lambda m, where_ref: (0, 0, 0, jnp.bitwise_xor(m, where_ref[0])),
                )
            ],
            out_specs=[pl.BlockSpec((2 * RANK, cols), lambda m, where_ref: (0, 0))] * (2 * per),
        ),
        out_shape=[jax.ShapeDtypeStruct((2 * RANK, cols), BF16)] * (2 * per),
        compiler_params=pltpu.CompilerParams(vmem_limit_bytes=VMEM_LIMIT),
        cost_estimate=pl.CostEstimate(
            flops=0, bytes_accessed=6 * adapters.size, transcendentals=0
        ),
        name="pieces",
    )(place, adapters)
    return pieces[:per], pieces[per:]


def spread(pieces, size):
    return [piece if m == 0 else exchange(piece, m, size) for m, piece in enumerate(pieces)]


def for_images_kernel(per, images, where_ref, ids_ref, *refs):
    piece_refs, (kept_ref, sent_ref) = refs[:per], refs[per:]
    zone, place = where_ref[0], where_ref[1]
    for r in range(images):
        tenant = ids_ref[jnp.bitwise_xor(zone, r)]
        block = jnp.zeros(piece_refs[0].shape, BF16)
        for m, piece_ref in enumerate(piece_refs):
            owner = zone * per + jnp.bitwise_xor(place, m)
            block = jnp.where(tenant == owner, piece_ref[...], block)
        if r % 2:
            sent_ref[r // 2] = block
        else:
            kept_ref[r // 2] = block


def for_images(where, tenant_ids, pieces):
    images = tenant_ids.shape[0]
    shape = (images // 2,) + pieces[0].shape
    smem = pl.BlockSpec(memory_space=pltpu.SMEM)
    return pl.pallas_call(
        functools.partial(for_images_kernel, len(pieces), images),
        in_specs=[smem, smem] + [pl.BlockSpec(memory_space=pltpu.VMEM)] * len(pieces),
        out_specs=[pl.BlockSpec(memory_space=pltpu.VMEM)] * 2,
        out_shape=[jax.ShapeDtypeStruct(shape, BF16)] * 2,
        compiler_params=pltpu.CompilerParams(vmem_limit_bytes=VMEM_LIMIT),
        cost_estimate=pl.CostEstimate(
            flops=0, bytes_accessed=8 * images * pieces[0].size, transcendentals=0
        ),
        name="for_images",
    )(where, tenant_ids, *pieces)


def halve_all(kept, came, per, size):
    blocks = [kept[i] + came[i] for i in range(kept.shape[0])]
    bit = 2
    while len(blocks) > 1:
        came = exchange(jnp.stack(blocks[1::2]), bit * per, size)
        blocks = [block + came[i] for i, block in enumerate(blocks[0::2])]
        bit *= 2
    return blocks[0]


def direct_images(slots, per, images, size):
    return [slots] + [exchange(slots, r * per, size) for r in range(1, images)]


def owner_kernel(per, images, where_ref, ids_ref, *refs):
    image_refs, sum_refs = refs[:images], refs[images:]
    zone, place = where_ref[0], where_ref[1]
    for m, sum_ref in enumerate(sum_refs):
        owner = zone * per + jnp.bitwise_xor(place, m)
        total = jnp.zeros(sum_ref.shape, F32)
        for r, image_ref in enumerate(image_refs):
            mine = ids_ref[jnp.bitwise_xor(zone, r)] == owner
            total = total + jnp.where(mine, image_ref[...].astype(F32), 0.0)
        sum_ref[...] = total.astype(sum_ref.dtype)


def owner_sums(where, tenant_ids, gathered, per, size):
    images = len(gathered)
    smem = pl.BlockSpec(memory_space=pltpu.SMEM)
    vmem = pl.BlockSpec(memory_space=pltpu.VMEM)
    sums = pl.pallas_call(
        functools.partial(owner_kernel, per, images),
        in_specs=[smem, smem] + [vmem] * images,
        out_specs=[vmem] * per,
        out_shape=[jax.ShapeDtypeStruct(gathered[0].shape, gathered[0].dtype)] * per,
        compiler_params=pltpu.CompilerParams(vmem_limit_bytes=VMEM_LIMIT),
        cost_estimate=pl.CostEstimate(
            flops=0, bytes_accessed=4 * images * gathered[0].size, transcendentals=0
        ),
        name="owner_sums",
    )(where, tenant_ids, *gathered)
    return [total if m == 0 else exchange(total, m, size) for m, total in enumerate(sums)]


def shards(
    tenant_ids,
    timesteps,
    counts,
    hidden_in,
    frozen_query,
    key_base,
    frozen_value,
    out_grad,
    adapters,
    first_moment,
    second_moment,
):
    images, rows, width = hidden_in.shape
    size = lax.axis_size("seq")
    per = size // images
    cols = width // per
    heads = HEADS // per
    length = size * rows
    me = lax.axis_index("seq")
    zone, place = me // per, me % per
    chunks = (heads - 1, 1)
    send_type = BF16

    hidden_sent = (
        hidden_in.reshape(images, rows, per, cols).transpose(0, 2, 1, 3).reshape(size, rows, cols)
    )
    hidden_sent, spread_from = tie(hidden_sent, adapters)
    pieces_a, pieces_b = column_pieces(place.reshape(1), spread_from, per)
    pieces_a = spread(pieces_a, size)
    hidden = lax.all_to_all(hidden_sent, "seq", 0, 0, tiled=True).reshape(length, cols)

    packed = pack(timesteps, frozen_query, key_base, frozen_value, out_grad, per, chunks)

    where = jnp.stack([zone, place])
    pieces_a, packed = tie(pieces_a, packed)
    a_kept, a_sent = for_images(where, tenant_ids, pieces_a)
    a_came = exchange(a_sent, per, size)
    b_kept, b_sent = for_images(where, tenant_ids, spread(pieces_b, size))
    a_rows = halve_all(a_kept, a_came, per, size)
    b_rows = halve_all(b_kept, exchange(b_sent, per, size), per, size)

    packed, a_rows = tie(packed, a_rows)
    u_total = reduce_scatter_rows(dot_nt(hidden, a_rows), place, per, size)

    u_rows = in_order(gather_rows(u_total, per, size), place)

    packed = list(packed)
    packed[-1], u_rows, b_rows = tie(packed[-1], u_rows, b_rows)

    partial_rows = None
    head = 0
    slots_b = []
    for sent, count in zip(packed, chunks):
        received = lax.all_to_all(sent, "seq", 0, 0, tiled=True).reshape(length, count * 4 * HD)
        partial_rows, slot = attend(received, u_rows, b_rows, partial_rows, head, send_type)
        slots_b.append(slot)
        head += count
    early = {0: jnp.concatenate(slots_b, axis=1)}
    bits = [1 << n for n in range(images.bit_length() - 1)]
    for bit in reversed(bits):
        early[bit] = exchange(early[0], bit * per, size)

    grad_total = reduce_scatter_rows(partial_rows, place, per, size)
    grad_rows = gather_rows(grad_total, per, size)
    late = slots_of_hidden(place.reshape(1), grad_rows, hidden, send_type)
    late, early[images // 2] = tie(late, early[images // 2])
    for r in range(1, images):
        if r not in early:
            low = r & -r
            early[r] = exchange(early[r ^ low], low * per, size)
    late = direct_images(late, per, images, size)
    early = owner_sums(where, tenant_ids, [early[r] for r in range(images)], per, size)
    early, late = tie(early, late)
    late = owner_sums(where, tenant_ids, late, per, size)
    return tuple(
        adam(place.reshape(1), counts, early, late, adapters, first_moment, second_moment)
    )


def solution(mesh):
    whole = P(("groups", "seq"), None, None, None)
    tokens = P("groups", "seq", None)
    in_specs = (P("groups"), P("groups"), P(("groups", "seq"))) + (tokens,) * 5 + (whole,) * 3
    return jax.shard_map(
        shards, mesh=mesh, in_specs=in_specs, out_specs=(whole,) * 3, check_vma=False
    )
```

```python
import functools
import math

import jax
import jax.numpy as jnp
from jax import lax
from jax.experimental import pallas as pl
from jax.experimental.pallas import tpu as pltpu
from jax.sharding import PartitionSpec as P

HEADS = 24
HD = 128
RANK = 64

adapter_scale = 0.5
norm_eps = 1e-06
beta_one = 0.9
beta_two = 0.999
adam_eps = 1e-08
learn_rate = 0.01
adam_step = 100.0
num_steps = 1000.0

SCORE_SCALE = HD ** (-0.5)
EXP_SCALE = SCORE_SCALE * math.log2(math.e)
VMEM_LIMIT = 24 << 20

F32 = jnp.float32
BF16 = jnp.bfloat16


def dot(left, right):
    return jnp.dot(left, right, preferred_element_type=F32)


def dot_nt(left, right):
    return lax.dot_general(left, right, (((1,), (1,)), ((), ())), preferred_element_type=F32)


def dot_tn(left, right):
    return lax.dot_general(left, right, (((0,), (0,)), ((), ())), preferred_element_type=F32)


def exchange(block, flip, size):
    return lax.ppermute(block, "seq", [(i, i ^ flip) for i in range(size)])


def pack_kernel(chunks, per, steps_ref, query_ref, key_ref, value_ref, grad_ref, *out_refs):
    step = jnp.full((query_ref.shape[1], HD), steps_ref[pl.program_id(0)], jnp.int32)
    weight = 1.0 / (((step.astype(F32) + 1.0) / num_steps) ** 2 + 0.25)
    head = 0
    for dest in range(per):
        for out_ref, count in zip(out_refs, chunks):
            for slot in range(count):
                cols = slice(head * HD, (head + 1) * HD)
                base = slot * 4 * HD
                key = key_ref[0, :, cols].astype(F32)
                inverse = lax.rsqrt(jnp.mean(key * key, axis=-1, keepdims=True) + norm_eps)
                out_ref[dest, :, base : base + HD] = query_ref[0, :, cols]
                out_ref[dest, :, base + HD : base + 2 * HD] = (key * inverse).astype(BF16)
                out_ref[dest, :, base + 2 * HD : base + 3 * HD] = value_ref[0, :, cols]
                out_ref[dest, :, base + 3 * HD : base + 4 * HD] = (
                    weight * grad_ref[0, :, cols].astype(F32)
                ).astype(BF16)
                head += 1


def pack(timesteps, frozen_query, key_base, frozen_value, out_grad, per, chunks):
    images, rows, width = frozen_query.shape
    spec = pl.BlockSpec((1, rows, width), lambda i: (i, 0, 0))
    return pl.pallas_call(
        functools.partial(pack_kernel, chunks, per),
        grid=(images,),
        in_specs=[pl.BlockSpec(memory_space=pltpu.SMEM)] + [spec] * 4,
        out_specs=[pl.BlockSpec((per, rows, n * 4 * HD), lambda i: (i, 0, 0)) for n in chunks],
        out_shape=[jax.ShapeDtypeStruct((images * per, rows, n * 4 * HD), BF16) for n in chunks],
        compiler_params=pltpu.CompilerParams(vmem_limit_bytes=50 << 20),
        cost_estimate=pl.CostEstimate(
            flops=0, bytes_accessed=16 * images * rows * width, transcendentals=0
        ),
        name="pack",
    )(timesteps, frozen_query, key_base, frozen_value, out_grad)


def attend_kernel(
    first, row_block, buf_ref, u_ref, bq_ref, bv_ref, *rest
):
    if first:
        gin_ref = None
    else:
        gin_ref, rest = rest[0], rest[1:]
    gout_ref, slot_ref, query_s, value_s, normed_s, inverse_s, dquery_s, dvalue_s, keyt_s = rest
    length = buf_ref.shape[0]

    @pl.when(pl.program_id(0) == 0)
    def _():
        gout_ref[...] = jnp.zeros_like(gout_ref) if first else gin_ref[...]

    query_raw = buf_ref[:, :HD].astype(F32) + adapter_scale * dot(u_ref[:, :RANK], bq_ref[...])
    inverse = lax.rsqrt(jnp.mean(query_raw * query_raw, axis=-1, keepdims=True) + norm_eps)
    normed = query_raw * inverse
    normed_s[...] = normed
    inverse_s[...] = jnp.broadcast_to(inverse, (length, HD))
    query_s[...] = normed.astype(BF16)
    value_s[...] = (
        buf_ref[:, 2 * HD : 3 * HD].astype(F32)
        + adapter_scale * dot(u_ref[:, RANK:], bv_ref[...])
    ).astype(BF16)
    key = buf_ref[:, HD : 2 * HD]
    keyt_s[...] = key.T
    for block in range(length // row_block):
        rows = slice(block * row_block, (block + 1) * row_block)
        upstream = buf_ref[rows, 3 * HD :]
        scores = dot_nt(key, query_s[rows, :])
        exp_scores = jnp.exp2(scores * EXP_SCALE)
        probs = exp_scores * (1.0 / jnp.sum(exp_scores, axis=0, keepdims=True))
        probs_b = probs.astype(BF16)
        dprobs = dot_nt(value_s[...], upstream)
        delta = jnp.sum(probs_b.astype(F32) * dprobs, axis=0, keepdims=True)
        dscores = (probs * (dprobs - delta)).astype(BF16)
        dquery_s[rows, :] = (dot(keyt_s[...], dscores) * SCORE_SCALE).T
        part = dot(probs_b, upstream)
        if block == 0:
            dvalue_s[...] = part
        else:
            dvalue_s[...] += part
    dquery_n = dquery_s[...].astype(BF16).astype(F32)
    normed = normed_s[...]
    dquery = (
        inverse_s[...]
        * (dquery_n - normed * jnp.mean(dquery_n * normed, axis=-1, keepdims=True))
    ).astype(BF16)
    dvalue = dvalue_s[...].astype(BF16)
    gout_ref[:, :RANK] += dot_nt(dquery, bq_ref[...])
    gout_ref[:, RANK:] += dot_nt(dvalue, bv_ref[...])
    slot_ref[:RANK, :] = (adapter_scale * dot_tn(u_ref[:, :RANK], dquery)).astype(slot_ref.dtype)
    slot_ref[RANK:, :] = (adapter_scale * dot_tn(u_ref[:, RANK:], dvalue)).astype(slot_ref.dtype)


def attend(received, u_rows, b_rows, partial_rows, first_head, send_type):
    length = received.shape[0]
    count = received.shape[1] // (4 * HD)
    first = partial_rows is None
    row_block = min(512, length)
    whole = lambda h: (0, 0)
    in_specs = [
        pl.BlockSpec((length, 4 * HD), lambda h: (0, h)),
        pl.BlockSpec((length, 2 * RANK), whole),
        pl.BlockSpec((RANK, HD), lambda h: (0, first_head + h)),
        pl.BlockSpec((RANK, HD), lambda h: (1, first_head + h)),
    ]
    operands = [received, u_rows, b_rows, b_rows]
    if not first:
        in_specs.append(pl.BlockSpec((length, 2 * RANK), whole))
        operands.append(partial_rows)
    return pl.pallas_call(
        functools.partial(attend_kernel, first, row_block),
        grid=(count,),
        in_specs=in_specs,
        out_specs=[
            pl.BlockSpec((length, 2 * RANK), whole),
            pl.BlockSpec((2 * RANK, HD), lambda h: (0, h)),
        ],
        out_shape=[
            jax.ShapeDtypeStruct((length, 2 * RANK), F32),
            jax.ShapeDtypeStruct((2 * RANK, count * HD), send_type),
        ],
        scratch_shapes=[
            pltpu.VMEM((length, HD), BF16),
            pltpu.VMEM((length, HD), BF16),
            pltpu.VMEM((length, HD), F32),
            pltpu.VMEM((length, HD), F32),
            pltpu.VMEM((length, HD), F32),
            pltpu.VMEM((length, HD), F32),
            pltpu.VMEM((HD, length), BF16),
        ],
        compiler_params=pltpu.CompilerParams(vmem_limit_bytes=VMEM_LIMIT),
        cost_estimate=pl.CostEstimate(
            flops=count * length * length * 10 * HD,
            bytes_accessed=2 * received.size,
            transcendentals=count * length * length,
        ),
        name="attend",
    )(*operands)


def adam_kernel(per, where_ref, count_ref, *refs):
    early_refs, late_refs, refs = refs[:per], refs[per : 2 * per], refs[2 * per :]
    adapter_ref, first_ref, second_ref, new_adapter_ref, new_first_ref, new_second_ref = refs
    first_corr = 1.0 - beta_one**adam_step
    second_corr = 1.0 - beta_two**adam_step
    share = 1.0 / count_ref[0].astype(F32)

    def step(mat, grad_ref):
        row = mat // 2 * RANK
        grad = grad_ref[row : row + RANK, :]
        grad = grad.astype(F32) * share
        new_first = beta_one * first_ref[0, mat] + (1.0 - beta_one) * grad
        new_second = beta_two * second_ref[0, mat] + (1.0 - beta_two) * grad * grad
        new_first_ref[0, mat] = new_first
        new_second_ref[0, mat] = new_second
        corrected = new_second * (1.0 / second_corr)
        root = corrected * lax.rsqrt(corrected)
        new_adapter_ref[0, mat] = adapter_ref[0, mat] - (learn_rate / first_corr) * new_first / (
            root + adam_eps
        )

    for m in range(per):

        @pl.when(pl.program_id(0) == m)
        def _(m=m):
            for half in range(2):
                step(2 * half, late_refs[m])
                step(2 * half + 1, early_refs[m])


def adam(place, counts, early, late, adapters, first_moment, second_moment):
    per = len(early)
    cols = adapters.shape[-1] // per
    state = pl.BlockSpec(
        (1, 4, RANK, cols),
        lambda m, where_ref, count_ref: (0, 0, 0, jnp.bitwise_xor(m, where_ref[0])),
    )
    grads = [
        pl.BlockSpec(grad.shape, lambda m, where_ref, count_ref: (0, 0))
        for grad in (*early, *late)
    ]
    return pl.pallas_call(
        functools.partial(adam_kernel, per),
        grid_spec=pltpu.PrefetchScalarGridSpec(
            num_scalar_prefetch=2,
            grid=(per,),
            in_specs=grads + [state] * 3,
            out_specs=[state] * 3,
        ),
        out_shape=[jax.ShapeDtypeStruct(adapters.shape, F32)] * 3,
        compiler_params=pltpu.CompilerParams(vmem_limit_bytes=VMEM_LIMIT),
        cost_estimate=pl.CostEstimate(
            flops=0, bytes_accessed=24 * adapters.size, transcendentals=0
        ),
        name="adam",
    )(place, counts, *early, *late, adapters, first_moment, second_moment)


def reduce_scatter_rows(partial, place, per, size):
    rows = partial.shape[0] // per
    total = lax.dynamic_slice_in_dim(partial, place * rows, rows, axis=0)
    came = [
        exchange(lax.dynamic_slice_in_dim(partial, (place ^ m) * rows, rows, axis=0), m, size)
        for m in range(1, per)
    ]
    for block in came:
        total = total + block
    return total.astype(BF16)


def gather_rows(total, per, size):
    return [total] + [exchange(total, m, size) for m in range(1, per)]


def in_order(blocks, place):
    bit = 1
    while bit < len(blocks):
        flip = (place & bit) != 0
        blocks = [
            jnp.where(flip, blocks[i ^ bit], blocks[i]) for i in range(len(blocks))
        ]
        bit *= 2
    return jnp.concatenate(blocks, axis=0)


def slot_kernel(per, where_ref, *refs):
    row_refs, (hidden_ref, out_ref, total_s) = refs[:per], refs[per:]
    for m, row_ref in enumerate(row_refs):

        @pl.when(pl.program_id(0) == m)
        def _(row_ref=row_ref, m=m):
            part = dot_tn(row_ref[...], hidden_ref[...])
            if m:
                part = part + total_s[...]
            if m < per - 1:
                total_s[...] = part
            else:
                out_ref[...] = (adapter_scale * part).astype(out_ref.dtype)


def slots_of_hidden(place, blocks, hidden, send_type):
    per = len(blocks)
    rows, width = blocks[0].shape
    cols = hidden.shape[1]
    whole = lambda m, where_ref: (0, 0)
    return pl.pallas_call(
        functools.partial(slot_kernel, per),
        grid_spec=pltpu.PrefetchScalarGridSpec(
            num_scalar_prefetch=1,
            grid=(per,),
            in_specs=[pl.BlockSpec((rows, width), whole)] * per
            + [pl.BlockSpec((rows, cols), lambda m, where_ref: (jnp.bitwise_xor(m, where_ref[0]), 0))],
            out_specs=pl.BlockSpec((width, cols), whole),
            scratch_shapes=[pltpu.VMEM((width, cols), F32)],
        ),
        out_shape=jax.ShapeDtypeStruct((width, cols), send_type),
        compiler_params=pltpu.CompilerParams(vmem_limit_bytes=VMEM_LIMIT),
        cost_estimate=pl.CostEstimate(
            flops=2 * rows * per * width * cols, bytes_accessed=2 * hidden.size, transcendentals=0
        ),
        name="slots",
    )(place, *blocks, hidden)


def tie(*values):
    return lax.optimization_barrier(values)


def pieces_kernel(per, where_ref, adapter_ref, *out_refs):
    for m in range(per):

        @pl.when(pl.program_id(0) == m)
        def _(m=m):
            for half in range(2):
                for row, mat in enumerate((half, half + 2)):
                    out_refs[half * per + m][row * RANK : (row + 1) * RANK, :] = adapter_ref[
                        0, mat
                    ].astype(BF16)


def column_pieces(place, adapters, per):
    cols = adapters.shape[-1] // per
    pieces = pl.pallas_call(
        functools.partial(pieces_kernel, per),
        grid_spec=pltpu.PrefetchScalarGridSpec(
            num_scalar_prefetch=1,
            grid=(per,),
            in_specs=[
                pl.BlockSpec(
                    (1, 4, RANK, cols),
                    lambda m, where_ref: (0, 0, 0, jnp.bitwise_xor(m, where_ref[0])),
                )
            ],
            out_specs=[pl.BlockSpec((2 * RANK, cols), lambda m, where_ref: (0, 0))] * (2 * per),
        ),
        out_shape=[jax.ShapeDtypeStruct((2 * RANK, cols), BF16)] * (2 * per),
        compiler_params=pltpu.CompilerParams(vmem_limit_bytes=VMEM_LIMIT),
        cost_estimate=pl.CostEstimate(
            flops=0, bytes_accessed=6 * adapters.size, transcendentals=0
        ),
        name="pieces",
    )(place, adapters)
    return pieces[:per], pieces[per:]


def spread(pieces, size):
    return [piece if m == 0 else exchange(piece, m, size) for m, piece in enumerate(pieces)]


def for_images_kernel(per, images, where_ref, ids_ref, *refs):
    piece_refs, (kept_ref, sent_ref) = refs[:per], refs[per:]
    zone, place = where_ref[0], where_ref[1]
    for r in range(images):
        tenant = ids_ref[jnp.bitwise_xor(zone, r)]
        block = jnp.zeros(piece_refs[0].shape, BF16)
        for m, piece_ref in enumerate(piece_refs):
            owner = zone * per + jnp.bitwise_xor(place, m)
            block = jnp.where(tenant == owner, piece_ref[...], block)
        if r % 2:
            sent_ref[r // 2] = block
        else:
            kept_ref[r // 2] = block


def for_images(where, tenant_ids, pieces):
    images = tenant_ids.shape[0]
    shape = (images // 2,) + pieces[0].shape
    smem = pl.BlockSpec(memory_space=pltpu.SMEM)
    return pl.pallas_call(
        functools.partial(for_images_kernel, len(pieces), images),
        in_specs=[smem, smem] + [pl.BlockSpec(memory_space=pltpu.VMEM)] * len(pieces),
        out_specs=[pl.BlockSpec(memory_space=pltpu.VMEM)] * 2,
        out_shape=[jax.ShapeDtypeStruct(shape, BF16)] * 2,
        compiler_params=pltpu.CompilerParams(vmem_limit_bytes=VMEM_LIMIT),
        cost_estimate=pl.CostEstimate(
            flops=0, bytes_accessed=8 * images * pieces[0].size, transcendentals=0
        ),
        name="for_images",
    )(where, tenant_ids, *pieces)


def halve_all(kept, came, per, size):
    blocks = [kept[i] + came[i] for i in range(kept.shape[0])]
    bit = 2
    while len(blocks) > 1:
        came = exchange(jnp.stack(blocks[1::2]), bit * per, size)
        blocks = [block + came[i] for i, block in enumerate(blocks[0::2])]
        bit *= 2
    return blocks[0]


def direct_images(slots, per, images, size):
    return [slots] + [exchange(slots, r * per, size) for r in range(1, images)]


def owner_kernel(per, images, where_ref, ids_ref, *refs):
    image_refs, sum_refs = refs[:images], refs[images:]
    zone, place = where_ref[0], where_ref[1]
    for m, sum_ref in enumerate(sum_refs):
        owner = zone * per + jnp.bitwise_xor(place, m)
        total = jnp.zeros(sum_ref.shape, F32)
        for r, image_ref in enumerate(image_refs):
            mine = ids_ref[jnp.bitwise_xor(zone, r)] == owner
            total = total + jnp.where(mine, image_ref[...].astype(F32), 0.0)
        sum_ref[...] = total.astype(sum_ref.dtype)


def owner_sums(where, tenant_ids, gathered, per, size):
    images = len(gathered)
    smem = pl.BlockSpec(memory_space=pltpu.SMEM)
    vmem = pl.BlockSpec(memory_space=pltpu.VMEM)
    sums = pl.pallas_call(
        functools.partial(owner_kernel, per, images),
        in_specs=[smem, smem] + [vmem] * images,
        out_specs=[vmem] * per,
        out_shape=[jax.ShapeDtypeStruct(gathered[0].shape, gathered[0].dtype)] * per,
        compiler_params=pltpu.CompilerParams(vmem_limit_bytes=VMEM_LIMIT),
        cost_estimate=pl.CostEstimate(
            flops=0, bytes_accessed=4 * images * gathered[0].size, transcendentals=0
        ),
        name="owner_sums",
    )(where, tenant_ids, *gathered)
    return [total if m == 0 else exchange(total, m, size) for m, total in enumerate(sums)]


def shards(
    tenant_ids,
    timesteps,
    counts,
    hidden_in,
    frozen_query,
    key_base,
    frozen_value,
    out_grad,
    adapters,
    first_moment,
    second_moment,
):
    images, rows, width = hidden_in.shape
    size = lax.axis_size("seq")
    per = size // images
    cols = width // per
    heads = HEADS // per
    length = size * rows
    me = lax.axis_index("seq")
    zone, place = me // per, me % per
    chunks = (heads - 1, 1)
    send_type = BF16

    hidden_sent = (
        hidden_in.reshape(images, rows, per, cols).transpose(0, 2, 1, 3).reshape(size, rows, cols)
    )
    hidden_sent, spread_from = tie(hidden_sent, adapters)
    pieces_a, pieces_b = column_pieces(place.reshape(1), spread_from, per)
    pieces_a = spread(pieces_a, size)
    hidden = lax.all_to_all(hidden_sent, "seq", 0, 0, tiled=True).reshape(length, cols)

    packed = pack(timesteps, frozen_query, key_base, frozen_value, out_grad, per, chunks)

    where = jnp.stack([zone, place])
    pieces_a, packed = tie(pieces_a, packed)
    a_kept, a_sent = for_images(where, tenant_ids, pieces_a)
    a_came = exchange(a_sent, per, size)
    b_kept, b_sent = for_images(where, tenant_ids, spread(pieces_b, size))
    a_rows = halve_all(a_kept, a_came, per, size)
    b_rows = halve_all(b_kept, exchange(b_sent, per, size), per, size)

    packed, a_rows = tie(packed, a_rows)
    u_total = reduce_scatter_rows(dot_nt(hidden, a_rows), place, per, size)

    u_rows = in_order(gather_rows(u_total, per, size), place)

    packed = list(packed)
    packed[-1], u_rows, b_rows = tie(packed[-1], u_rows, b_rows)

    partial_rows = None
    head = 0
    slots_b = []
    for sent, count in zip(packed, chunks):
        received = lax.all_to_all(sent, "seq", 0, 0, tiled=True).reshape(length, count * 4 * HD)
        partial_rows, slot = attend(received, u_rows, b_rows, partial_rows, head, send_type)
        slots_b.append(slot)
        head += count
    early = {0: jnp.concatenate(slots_b, axis=1)}
    bits = [1 << n for n in range(images.bit_length() - 1)]
    for bit in reversed(bits):
        early[bit] = exchange(early[0], bit * per, size)

    grad_total = reduce_scatter_rows(partial_rows, place, per, size)
    grad_rows = gather_rows(grad_total, per, size)
    late = slots_of_hidden(place.reshape(1), grad_rows, hidden, send_type)
    late, early[images // 2] = tie(late, early[images // 2])
    for r in range(1, images):
        if r not in early:
            low = r & -r
            early[r] = exchange(early[r ^ low], low * per, size)
    late = direct_images(late, per, images, size)
    early = owner_sums(where, tenant_ids, [early[r] for r in range(images)], per, size)
    early[1], late = tie(early[1], late)
    late = owner_sums(where, tenant_ids, late, per, size)
    return tuple(
        adam(place.reshape(1), counts, early, late, adapters, first_moment, second_moment)
    )


def solution(mesh):
    whole = P(("groups", "seq"), None, None, None)
    tokens = P("groups", "seq", None)
    in_specs = (P("groups"), P("groups"), P(("groups", "seq"))) + (tokens,) * 5 + (whole,) * 3
    return jax.shard_map(
        shards, mesh=mesh, in_specs=in_specs, out_specs=(whole,) * 3, check_vma=False
    )
```
